512 devices in a mesh: dp: 32 (over z, core), tensor: 16 (over y, x).
Axes of the slice: x: 4, y: 4, z: 16, core: 2. Of those that a mesh axis runs over, the one named last changes fastest.
Arguments:
- hidden: bfloat16 [4096, 18432], P('dp', 'tensor'), may hold values from -80 to 80
- out_grad: bfloat16 [4096, 4608], P('dp'), may hold values from -80 to 80
- live: int32 [32], P('dp'), may hold values 0 or 1
Outputs:
- clipped_grad: float32 [18432, 4608], P('tensor', 'dp')
- norms: float32 [32], P('dp')
The draws below stay inside these ranges and needn't reach their ends.
All inputs are finite; a program needn't handle non-finite values. No bound on the sum of `live` on one device may be relied on, other than what follows from the above.
Results may differ from the reference program's by a relative error of at most 0.0021.
Values may be sent and summed in bfloat16 or wider, within the bound.
No kernel may reach another device: no remote copies, remote signals or barrier semaphores. Data moves between devices by JAX's collectives and lax.ppermute only.
A program may use at most 64 MiB of HBM per device.

```python
import math
import jax
import jax.numpy as jnp
from jax import lax

D = 4608
UNITS = 18432
SEQ = 128
N_DP = 32


def topic_labels(key):
    return jax.random.randint(jax.random.fold_in(key, 5), (N_DP * SEQ,), 0, 8)


def topic_part(key, labels, width):
    share = min(1.0, (8.0 / SEQ) ** 0.25)
    topics = jnp.clip(jax.random.normal(key, (N_DP, 8, width), jnp.float32), -5.0, 5.0)
    sequence_index = jnp.arange(N_DP * SEQ) // SEQ
    return share * topics[sequence_index, labels]


def draw_hidden(key, part):
    labels = topic_labels(key)
    key = jax.random.fold_in(key, 11)
    first, second, third = jax.random.split(key, 3)
    columns = jnp.arange(UNITS, dtype=jnp.float32) / UNITS
    scale = jnp.exp(jnp.log(3.0) * columns + jax.random.uniform(second, (UNITS,), jnp.float32, -0.5, 0.5))
    base = jnp.clip(jax.random.normal(first, (N_DP * SEQ, UNITS), jnp.float32), -5.0, 5.0)
    mixed = base + topic_part(third, labels, UNITS)
    return (mixed * scale[None, :]).astype(jnp.bfloat16)


def draw_out_grad(key, part):
    labels = topic_labels(key)
    key = jax.random.fold_in(key, 23)
    first, second, third, fourth = jax.random.split(key, 4)
    rows_scale = jnp.exp(jax.random.uniform(second, (N_DP, 1), jnp.float32, jnp.log(0.05), jnp.log(1.5)))
    columns = jnp.arange(D, dtype=jnp.float32) / D
    cols_scale = jnp.exp(jnp.log(3.0) * columns + jax.random.uniform(third, (D,), jnp.float32, -0.5, 0.5))
    base = jnp.clip(jax.random.normal(first, (N_DP * SEQ, D), jnp.float32), -5.0, 5.0)
    mixed = (base + topic_part(fourth, labels, D)).reshape(N_DP, SEQ, D)
    shaped = mixed * rows_scale[:, :, None] * cols_scale[None, None, :]
    return shaped.reshape(N_DP * SEQ, D).astype(jnp.bfloat16)


def with_ends(values, key, low, top_value):
    place = [jax.random.randint(jax.random.fold_in(key, axis), (), 0, length) for axis, length in enumerate(values.shape)]
    longest = values.shape.index(max(values.shape))
    beside = place[:longest] + [(place[longest] + 1) % values.shape[longest]] + place[longest + 1:]
    return values.at[tuple(place)].set(low).at[tuple(beside)].set(top_value)


def setup_inputs(seed: int = 0) -> dict:
    keys = jax.random.split(jax.random.key(seed), 4)
    hidden = draw_hidden(jax.random.fold_in(keys[3], 71), 0)
    out_grad = draw_out_grad(jax.random.fold_in(keys[3], 71), 0)
    live = with_ends((jax.random.randint(keys[2], (N_DP,), 0, 16) < 15).astype(jnp.int32), jax.random.fold_in(keys[2], 1), 0, 1)
    return {"hidden": hidden, "out_grad": out_grad, "live": live}


def sequence_norm(pair):
    rows_h, rows_g = pair
    gram_h = jnp.dot(rows_h, rows_h.T, preferred_element_type=jnp.float32)
    gram_g = jnp.dot(rows_g, rows_g.T, preferred_element_type=jnp.float32)
    return jnp.sum(gram_h * gram_g)

def reference(hidden, out_grad, live):
    stacked_h = hidden.reshape(N_DP, SEQ, UNITS)
    stacked_g = out_grad.reshape(N_DP, SEQ, D)
    totals = lax.map(sequence_norm, (stacked_h, stacked_g))
    q_values = totals / (float(SEQ) * float(UNITS) * float(D))
    norms = jnp.sqrt(q_values)
    clip = live.astype(jnp.float32) * jnp.minimum(1.0, 1.0 / jnp.sqrt(q_values + 1e-06))
    scaled = (stacked_g.astype(jnp.float32) * clip[:, None, None]).astype(jnp.bfloat16).reshape(N_DP * SEQ, D)
    grad = lax.dot_general(hidden, scaled, (((0,), (0,)), ((), ())), preferred_element_type=jnp.float32)
    grad = grad / math.sqrt(N_DP * SEQ)
    return (grad, norms)
```

```python
import math

import jax
import jax.numpy as jnp
from jax import lax
from jax.experimental import pallas as pl
from jax.experimental.pallas import tpu as pltpu
from jax.sharding import Mesh, PartitionSpec as P

D = 4608
UNITS = 18432
SEQ = 128
NZ, NC, NY, NX = 16, 2, 4, 4
NT = NY * NX
CHIP = D // NZ
OWN = CHIP // NC
TAIL = 16
HOPS = NZ // 2

LINE = ("z", "core")
PLANE = ("y", "x")
ALL = ("z", "core", "y", "x")
STEP = [(z * 2, (z + 1) % NZ * 2) for z in range(NZ)]
STEP += [(z * 2 + 1, (z - 1) % NZ * 2 + 1) for z in range(NZ)]
SWAP = [(0, 1), (1, 0)]


def spread_pairs():
    pairs = []
    for z in range(NZ):
        for c in range(NC):
            for t in range(NT):
                to_z = (z + t if c == 0 else z - t) % NZ
                to_c = c if t <= HOPS else 1 - c
                pairs.append(((z * NC + c) * NT + t, (to_z * NC + to_c) * NT + t))
    return pairs


def vmem():
    return pl.BlockSpec(memory_space=pltpu.VMEM)


def smem():
    return pl.BlockSpec(memory_space=pltpu.SMEM)


def call(kernel, outs, ins, name, flops, scratch=(), aliases=None):
    moved = sum(math.prod(a.shape) * a.dtype.itemsize for a in list(ins) + list(outs))
    return pl.pallas_call(
        kernel,
        out_shape=outs,
        in_specs=[smem() if a.dtype == jnp.int32 else vmem() for a in ins],
        out_specs=[vmem() for _ in outs],
        scratch_shapes=list(scratch),
        input_output_aliases=aliases or {},
        compiler_params=pltpu.CompilerParams(vmem_limit_bytes=40 * 1024 * 1024),
        cost_estimate=pl.CostEstimate(flops=flops, bytes_accessed=moved, transcendentals=0),
        name=name,
    )(*ins)


def gram_kernel(h_ref, g_ref, p_ref):
    dims = (((1,), (1,)), ((), ()))
    h, g = h_ref[...], g_ref[...]
    gram_h = lax.dot_general(h, h, dims, preferred_element_type=jnp.float32)
    gram_g = lax.dot_general(g, g, dims, preferred_element_type=jnp.float32)
    p_ref[...] = jnp.full(p_ref.shape, jnp.sum(gram_h * gram_g), jnp.float32)


def pack_kernel(to_ref, g_ref, out_ref, turned):
    start = to_ref[0] * CHIP
    base = pl.multiple_of(start // 128 * 128, 128)
    window = g_ref[:, pl.ds(base, 384)].astype(jnp.float32)
    turned[...] = window.T
    out_ref[...] = turned[pl.ds(pl.multiple_of(start - base, 32), CHIP), :].astype(jnp.bfloat16)


def bundle_kernel(own_ref, other_ref, block_ref, out_ref):
    sub = lax.broadcasted_iota(jnp.int32, (NZ, 128), 0)
    lane = lax.broadcasted_iota(jnp.int32, (NZ, 128), 1)

    def in_lanes(row):
        mine = jnp.where(lane == sub, own_ref[:, row, :], 0.0)
        others = jnp.where(lane == sub + NZ, other_ref[:, row, :], 0.0)
        return jnp.sum(mine + others, axis=0, keepdims=True)

    part, live = in_lanes(0), in_lanes(1)
    high = part.astype(jnp.bfloat16).astype(jnp.float32)
    middle = (part - high).astype(jnp.bfloat16).astype(jnp.float32)
    low = part - high - middle
    rows = lax.broadcasted_iota(jnp.int32, (TAIL, 128), 0)
    tail = jnp.where(rows == 0, high, jnp.where(rows == 1, middle, jnp.where(rows == 2, low, jnp.where(rows == 3, live, 0.0))))
    tail = tail.astype(jnp.bfloat16)
    block = block_ref[...]
    for t in range(NT):
        out_ref[t, 0:CHIP, :] = block
        out_ref[t, CHIP:CHIP + TAIL, :] = tail


def scale_kernel(at_ref, got_ref, s_ref, norm_ref):
    z, core = at_ref[0], at_ref[1]
    sign = 1 - 2 * core
    tails = got_ref[:, CHIP:CHIP + TAIL, :].astype(jnp.float32)
    total = jnp.sum(tails, axis=0)
    q = (total[0:1] + total[1:2] + total[2:3]) / (float(SEQ) * float(UNITS) * float(D))
    live = tails[0, 3:4, :]
    clip = live * jnp.minimum(1.0, 1.0 / jnp.sqrt(q + 1e-06))
    lane = lax.broadcasted_iota(jnp.int32, (1, 128), 1)

    def pick(row, at):
        return jnp.sum(jnp.where(lane == at, row, 0.0), axis=1, keepdims=True)

    norm_ref[...] = jnp.broadcast_to(pick(jnp.sqrt(q), z), norm_ref.shape)
    own = pl.multiple_of(core * OWN, 16)
    other = pl.multiple_of((1 - core) * OWN, 16)
    for t in range(NT):
        hops = t if t <= HOPS else NZ - t
        at = lax.rem(z - sign * hops + NZ, NZ) + (0 if t <= HOPS else NZ)
        factor = pick(clip, at)
        s_ref[t, 0:OWN, :] = (got_ref[t, pl.ds(own, OWN), :].astype(jnp.float32) * factor).astype(jnp.bfloat16)
        s_ref[t, OWN:CHIP, :] = (got_ref[t, pl.ds(other, OWN), :].astype(jnp.float32) * factor).astype(jnp.bfloat16)


def product(s_ref, hop, p, q):
    if q is None:
        return jnp.dot(s_ref[hop], p[...], preferred_element_type=jnp.float32)
    left = jnp.concatenate([s_ref[hop], s_ref[NZ - hop]], axis=1)
    right = jnp.concatenate([p[...], q[...]], axis=0)
    return jnp.dot(left, right, preferred_element_type=jnp.float32)


def matmul(s, hops, ps, qs, acc, last):
    blocks = [b for hop in hops for b in (ps[hop], qs[hop]) if b is not None]
    ins = [s] + blocks + ([acc] if acc is not None else [])
    units = blocks[0].shape[1]

    def kernel(*refs):
        s_ref, rest = refs[0], list(refs[1:])
        taken = [(hop, rest.pop(0), rest.pop(0) if qs[hop] is not None else None) for hop in hops]
        total = rest.pop(0)[...] if acc is not None else None
        for hop, p, q in taken:
            term = product(s_ref, hop, p, q)
            total = term if total is None else total + term
        if last:
            rest[0][...] = total[0:OWN]
            rest[1][...] = total[OWN:CHIP]
        else:
            rest[0][...] = total

    if last:
        outs = [jax.ShapeDtypeStruct((OWN, units), jnp.float32)] * 2
    else:
        outs = [jax.ShapeDtypeStruct((CHIP, units), jnp.float32)]
    flops = 2 * CHIP * units * SEQ * len(blocks)
    return call(kernel, outs, ins, "products", flops)


def per_device(hidden, out_grad, live):
    z, core = lax.axis_index("z"), lax.axis_index("core")
    t = lax.axis_index(PLANE)
    units = hidden.shape[1]

    ps, qs = [hidden], [None]
    p, q = hidden, None
    p = lax.ppermute(p, LINE, STEP)
    q = lax.ppermute(hidden, "core", SWAP)
    ps.append(p)
    for hop in range(1, HOPS):
        q = lax.ppermute(q, LINE, STEP)
        qs.append(q)
        p = lax.ppermute(p, LINE, STEP)
        ps.append(p)
    qs.append(None)

    to = lax.rem(z + (1 - 2 * core) * t + NZ, NZ).astype(jnp.int32).reshape(1)
    [block] = call(pack_kernel, [jax.ShapeDtypeStruct((CHIP, SEQ), jnp.bfloat16)], [to, out_grad], "pack", 0,
                   scratch=[pltpu.VMEM((384, SEQ), jnp.float32)])
    block = lax.ppermute(block, ALL, spread_pairs())

    [part] = call(gram_kernel, [jax.ShapeDtypeStruct((8, 128), jnp.float32)], [hidden, out_grad], "grams",
                  2 * SEQ * SEQ * (units + D))
    row = lax.broadcasted_iota(jnp.int32, (8, 128), 0)
    part = jnp.where(row == 0, part, jnp.where(row == 1, live.astype(jnp.float32)[0], 0.0))
    parts = lax.all_to_all(jnp.broadcast_to(part[None], (NZ, 8, 128)), "z", 0, 0, tiled=True)
    others = lax.ppermute(parts, "core", SWAP)

    [bundle] = call(bundle_kernel, [jax.ShapeDtypeStruct((NT, CHIP + TAIL, SEQ), jnp.bfloat16)], [parts, others, block], "bundle", 0)
    got = lax.all_to_all(bundle, PLANE, 0, 0, tiled=False)

    at = jnp.stack([z, core]).astype(jnp.int32)
    s, norm = call(scale_kernel, [jax.ShapeDtypeStruct((NT, CHIP, SEQ), jnp.bfloat16), jax.ShapeDtypeStruct((8, 128), jnp.float32)],
                   [at, got], "scale", 0)

    [acc] = matmul(s, range(0, 6), ps, qs, None, False)
    [acc] = matmul(s, range(6, 8), ps, qs, acc, False)
    mine, theirs = matmul(s, range(8, 9), ps, qs, acc, True)
    total = mine + lax.ppermute(theirs, "core", SWAP)
    grad = (total / math.sqrt(NZ * NC * SEQ)).T
    return grad, norm[0, 0:1]


def solution(mesh):
    grid = Mesh(mesh.devices.reshape(NZ, NC, NY, NX), ALL)
    return jax.shard_map(
        per_device,
        mesh=grid,
        in_specs=(P(LINE, PLANE), P(LINE, None), P(LINE)),
        out_specs=(P(PLANE, LINE), P(LINE)),
        check_vma=False,
    )
```

```python
import math

import jax
import jax.numpy as jnp
from jax import lax
from jax.experimental import pallas as pl
from jax.experimental.pallas import tpu as pltpu
from jax.sharding import Mesh, PartitionSpec as P

D = 4608
UNITS = 18432
SEQ = 128
NZ, NC, NY, NX = 16, 2, 4, 4
NT = NY * NX
CHIP = D // NZ
OWN = CHIP // NC
HOPS = NZ // 2

LINE = ("z", "core")
PLANE = ("y", "x")
ALL = ("z", "core", "y", "x")
SWAP = [(0, 1), (1, 0)]


def spread_pairs():
    pairs = []
    for z in range(NZ):
        for c in range(NC):
            for t in range(NT):
                to = (z + t if c == 0 else z - t) % NZ
                pairs.append(((z * NC + c) * NT + t, (to * NC + c) * NT + t))
    return pairs


def vmem():
    return pl.BlockSpec(memory_space=pltpu.VMEM)


def smem():
    return pl.BlockSpec(memory_space=pltpu.SMEM)


def call(kernel, outs, ins, name, flops, scratch=(), far=False):
    moved = sum(math.prod(a.shape) * a.dtype.itemsize for a in list(ins) + list(outs))
    return pl.pallas_call(
        kernel,
        out_shape=outs,
        in_specs=[smem() if a.dtype == jnp.int32 else pl.BlockSpec(memory_space=pl.ANY) if far else vmem() for a in ins],
        out_specs=[vmem() for _ in outs],
        scratch_shapes=list(scratch),
        compiler_params=pltpu.CompilerParams(vmem_limit_bytes=16 * 1024 * 1024),
        cost_estimate=pl.CostEstimate(flops=flops, bytes_accessed=moved, transcendentals=0),
        name=name,
    )(*ins)


def gram_kernel(to_ref, h_hbm, g_hbm, part_ref, turned_ref, h_ref, g_ref, turned, h_sem, g_sem):
    h_copy = pltpu.make_async_copy(h_hbm, h_ref, h_sem)
    g_copy = pltpu.make_async_copy(g_hbm, g_ref, g_sem)
    h_copy.start()
    g_copy.start()
    dims = (((1,), (1,)), ((), ()))
    h_copy.wait()
    gram_h = lax.dot_general(h_ref[...], h_ref[...], dims, preferred_element_type=jnp.float32)
    g_copy.wait()
    gram_g = lax.dot_general(g_ref[...], g_ref[...], dims, preferred_element_type=jnp.float32)
    part_ref[...] = jnp.full(part_ref.shape, jnp.sum(gram_h * gram_g), jnp.float32)
    start = to_ref[0] * CHIP
    base = pl.multiple_of(start // 128 * 128, 128)
    turned[...] = g_ref[:, pl.ds(base, 384)].astype(jnp.float32).T
    turned_ref[...] = turned[pl.ds(pl.multiple_of(start - base, 32), CHIP), :]


def clip_kernel(live_ref, parts_ref, turned_ref, block_ref, norm_ref):
    total = jnp.sum(parts_ref[...], axis=0)[0:1, :]
    q = total / (float(SEQ) * float(UNITS) * float(D))
    live = live_ref[0].astype(jnp.float32)
    clip = live * jnp.minimum(1.0, 1.0 / jnp.sqrt(q + 1e-06))
    norm_ref[...] = jnp.broadcast_to(jnp.sqrt(q), norm_ref.shape)
    block_ref[...] = (turned_ref[...] * clip).astype(jnp.bfloat16)


def spread_kernel(block_ref, out_ref):
    block = block_ref[...]
    for t in range(NT):
        out_ref[t] = block


def product_kernel(at_ref, s_ref, h_ref, mine_ref, theirs_ref, total_ref):
    z, core = at_ref[0], at_ref[1]
    sign = 1 - 2 * core
    step = pl.program_id(0)

    def columns(of):
        return s_ref[lax.rem(sign * (z - of) + NZ, NZ)]

    left = jnp.concatenate([columns(2 * step), columns(2 * step + 1)], axis=1)
    right = h_ref[...].reshape(2 * SEQ, h_ref.shape[2])
    term = jnp.dot(left, right, preferred_element_type=jnp.float32)

    @pl.when(step == 0)
    def _():
        total_ref[...] = term

    @pl.when(step > 0)
    def _():
        total_ref[...] += term

    @pl.when(step == NZ // 2 - 1)
    def _():
        mine_ref[...] = total_ref[pl.ds(pl.multiple_of(core * OWN, 8), OWN), :]
        theirs_ref[...] = total_ref[pl.ds(pl.multiple_of((1 - core) * OWN, 8), OWN), :]


def products(at, s, gathered):
    units = gathered.shape[2]
    half = jax.ShapeDtypeStruct((OWN, units), jnp.float32)
    return pl.pallas_call(
        product_kernel,
        out_shape=[half, half],
        grid=(NZ // 2,),
        in_specs=[smem(), vmem(), pl.BlockSpec((2, SEQ, units), lambda i: (i, 0, 0))],
        out_specs=[vmem(), vmem()],
        scratch_shapes=[pltpu.VMEM((CHIP, units), jnp.float32)],
        compiler_params=pltpu.CompilerParams(vmem_limit_bytes=16 * 1024 * 1024),
        cost_estimate=pl.CostEstimate(
            flops=2 * CHIP * units * NZ * SEQ,
            bytes_accessed=gathered.size * 2 + s.size * 2 + 8 * OWN * units,
            transcendentals=0,
        ),
        name="products",
    )(at, s, gathered)


def per_device(hidden, out_grad, live):
    z, core = lax.axis_index("z"), lax.axis_index("core")
    t = lax.axis_index(PLANE)
    units = hidden.shape[1]
    gathered = lax.all_gather(hidden, "z", axis=0, tiled=False)

    to = lax.rem(z + (1 - 2 * core) * t + NZ, NZ).astype(jnp.int32).reshape(1)
    part, turned = call(
        gram_kernel,
        [jax.ShapeDtypeStruct((NT, 8, 128), jnp.float32), jax.ShapeDtypeStruct((CHIP, SEQ), jnp.float32)],
        [to, hidden, out_grad], "grams", 2 * SEQ * SEQ * (units + D),
        scratch=[pltpu.VMEM(hidden.shape, hidden.dtype), pltpu.VMEM(out_grad.shape, out_grad.dtype),
                 pltpu.VMEM((384, SEQ), jnp.float32), pltpu.SemaphoreType.DMA, pltpu.SemaphoreType.DMA],
        far=True,
    )
    parts = lax.all_to_all(part, PLANE, 0, 0, tiled=False)
    block, norm = call(
        clip_kernel,
        [jax.ShapeDtypeStruct((CHIP, SEQ), jnp.bfloat16), jax.ShapeDtypeStruct((8, 128), jnp.float32)],
        [live, parts, turned], "clip", 0,
    )
    block = lax.ppermute(block, ALL, spread_pairs())
    [spread] = call(spread_kernel, [jax.ShapeDtypeStruct((NT, CHIP, SEQ), jnp.bfloat16)], [block], "spread", 0)
    s = lax.all_to_all(spread, PLANE, 0, 0, tiled=False)

    mine, theirs = products(jnp.stack([z, core]).astype(jnp.int32), s, gathered)
    total = mine + lax.ppermute(theirs, "core", SWAP)
    grad = (total / math.sqrt(NZ * NC * SEQ)).T
    return grad, norm[0, 0:1]


def solution(mesh):
    grid = Mesh(mesh.devices.reshape(NZ, NC, NY, NX), ALL)
    return jax.shard_map(
        per_device,
        mesh=grid,
        in_specs=(P(LINE, PLANE), P(LINE, None), P(LINE)),
        out_specs=(P(PLANE, LINE), P(LINE)),
        check_vma=False,
    )
```

```python
import math

import jax
import jax.numpy as jnp
from jax import lax
from jax.experimental import pallas as pl
from jax.experimental.pallas import tpu as pltpu
from jax.sharding import Mesh, PartitionSpec as P

D = 4608
UNITS = 18432
SEQ = 128
NZ, NC, NY, NX = 16, 2, 4, 4
NT = NY * NX
CHIP = D // NZ
OWN = CHIP // NC
HOPS = NZ // 2

LINE = ("z", "core")
PLANE = ("y", "x")
ALL = ("z", "core", "y", "x")
STEP = [(z * 2, (z + 1) % NZ * 2) for z in range(NZ)]
STEP += [(z * 2 + 1, (z - 1) % NZ * 2 + 1) for z in range(NZ)]
SWAP = [(0, 1), (1, 0)]


def spread_pairs():
    pairs = []
    for z in range(NZ):
        for c in range(NC):
            for t in range(NT):
                to_z = (z + t if c == 0 else z - t) % NZ
                to_c = c if t <= HOPS else 1 - c
                pairs.append(((z * NC + c) * NT + t, (to_z * NC + to_c) * NT + t))
    return pairs


def vmem():
    return pl.BlockSpec(memory_space=pltpu.VMEM)


def smem():
    return pl.BlockSpec(memory_space=pltpu.SMEM)


def call(kernel, outs, ins, name, flops, scratch=(), far=False, tokens=()):
    moved = sum(math.prod(a.shape) * a.dtype.itemsize for a in list(ins) + list(outs))
    if tokens:
        inner, n = kernel, len(ins)

        def kernel(*refs):
            inner(*refs[:n], *refs[n + len(tokens):])

    return pl.pallas_call(
        kernel,
        out_shape=outs,
        in_specs=[smem() if a.dtype == jnp.int32 else pl.BlockSpec(memory_space=pl.ANY) if far else vmem() for a in ins]
        + [pl.BlockSpec(memory_space=pl.ANY) for _ in tokens],
        out_specs=[vmem() for _ in outs],
        scratch_shapes=list(scratch),
        compiler_params=pltpu.CompilerParams(vmem_limit_bytes=16 * 1024 * 1024),
        cost_estimate=pl.CostEstimate(flops=flops, bytes_accessed=moved, transcendentals=0),
        name=name,
    )(*ins, *tokens)


def after(x, *others, cost=0):
    def kernel(*refs):
        del refs

    return pl.pallas_call(
        kernel,
        out_shape=jax.ShapeDtypeStruct(x.shape, x.dtype),
        in_specs=[pl.BlockSpec(memory_space=pl.ANY)] * (1 + len(others)),
        out_specs=pl.BlockSpec(memory_space=pl.ANY),
        input_output_aliases={0: 0},
        compiler_params=pltpu.CompilerParams(vmem_limit_bytes=1024 * 1024),
        cost_estimate=pl.CostEstimate(flops=cost, bytes_accessed=0, transcendentals=0),
        name="after",
    )(x, *others)


def gram_kernel(to_ref, h_hbm, g_hbm, part_ref, turned_ref, h_ref, g_ref, turned, h_sem, g_sem):
    h_copy = pltpu.make_async_copy(h_hbm, h_ref, h_sem)
    g_copy = pltpu.make_async_copy(g_hbm, g_ref, g_sem)
    h_copy.start()
    g_copy.start()
    dims = (((1,), (1,)), ((), ()))
    h_copy.wait()
    gram_h = lax.dot_general(h_ref[...], h_ref[...], dims, preferred_element_type=jnp.float32)
    g_copy.wait()
    gram_g = lax.dot_general(g_ref[...], g_ref[...], dims, preferred_element_type=jnp.float32)
    part_ref[...] = jnp.full(part_ref.shape, jnp.sum(gram_h * gram_g), jnp.float32)
    start = to_ref[0] * CHIP
    base = pl.multiple_of(start // 128 * 128, 128)
    turned[...] = g_ref[:, pl.ds(base, 384)].astype(jnp.float32).T
    turned_ref[...] = turned[pl.ds(pl.multiple_of(start - base, 32), CHIP), :]


def clip_kernel(live_ref, parts_ref, turned_ref, block_ref, norm_ref):
    total = jnp.sum(parts_ref[...], axis=0)[0:1, :]
    q = total / (float(SEQ) * float(UNITS) * float(D))
    live = live_ref[0].astype(jnp.float32)
    clip = live * jnp.minimum(1.0, 1.0 / jnp.sqrt(q + 1e-06))
    norm_ref[...] = jnp.broadcast_to(jnp.sqrt(q), norm_ref.shape)
    block_ref[...] = (turned_ref[...] * clip).astype(jnp.bfloat16)


def spread_kernel(block_ref, out_ref):
    block = block_ref[...]
    for t in range(NT):
        out_ref[t] = block


def product(s_ref, hop, p, q):
    if q is None:
        return jnp.dot(s_ref[hop], p[...], preferred_element_type=jnp.float32)
    left = jnp.concatenate([s_ref[hop], s_ref[NZ - hop]], axis=1)
    right = jnp.concatenate([p[...], q[...]], axis=0)
    return jnp.dot(left, right, preferred_element_type=jnp.float32)


def matmul(s, hops, ps, qs, acc, core=None):
    blocks = [b for hop in hops for b in (ps[hop], qs[hop]) if b is not None]
    ins = [s] + blocks + ([acc] if acc is not None else []) + ([core] if core is not None else [])
    units = blocks[0].shape[1]

    def kernel(*refs):
        s_ref, rest = refs[0], list(refs[1:])
        taken = [(hop, rest.pop(0), rest.pop(0) if qs[hop] is not None else None) for hop in hops]
        total = rest.pop(0)[...] if acc is not None else None
        for hop, p, q in taken:
            term = product(s_ref, hop, p, q)
            total = term if total is None else total + term
        if core is None:
            rest[0][...] = total
            return
        core_ref, mine_ref, theirs_ref, total_ref = rest
        total_ref[...] = total
        mine_ref[...] = total_ref[pl.ds(pl.multiple_of(core_ref[0] * OWN, 8), OWN), :]
        theirs_ref[...] = total_ref[pl.ds(pl.multiple_of((1 - core_ref[0]) * OWN, 8), OWN), :]

    whole = jax.ShapeDtypeStruct((CHIP, units), jnp.float32)
    half = jax.ShapeDtypeStruct((OWN, units), jnp.float32)
    flops = 2 * CHIP * units * SEQ * len(blocks)
    if core is None:
        return call(kernel, [whole], ins, "products", flops)
    return call(kernel, [half, half], ins, "products", flops, scratch=[pltpu.VMEM(whole.shape, whole.dtype)])


def per_device(hidden, out_grad, live):
    z, core = lax.axis_index("z"), lax.axis_index("core")
    t = lax.axis_index(PLANE)
    units = hidden.shape[1]

    ps, qs = [hidden], [None]
    own_q = lax.ppermute(hidden, "core", SWAP)

    def advance(hop):
        if hop < HOPS:
            qs.append(lax.ppermute(qs[-1] if hop > 1 else own_q, LINE, STEP))
        else:
            qs.append(None)
        ps.append(lax.ppermute(ps[-1], LINE, STEP))

    advance(1)

    to = lax.rem(z + (1 - 2 * core) * t + NZ, NZ).astype(jnp.int32).reshape(1)
    part, turned = call(
        gram_kernel,
        [jax.ShapeDtypeStruct((NT, 8, 128), jnp.float32), jax.ShapeDtypeStruct((CHIP, SEQ), jnp.float32)],
        [to, hidden, out_grad], "grams", 2 * SEQ * SEQ * (units + D),
        scratch=[pltpu.VMEM(hidden.shape, hidden.dtype), pltpu.VMEM(out_grad.shape, out_grad.dtype),
                 pltpu.VMEM((384, SEQ), jnp.float32), pltpu.SemaphoreType.DMA, pltpu.SemaphoreType.DMA],
        far=True,
    )
    def clipped(parts):
        return call(
            clip_kernel,
            [jax.ShapeDtypeStruct((CHIP, SEQ), jnp.bfloat16), jax.ShapeDtypeStruct((8, 128), jnp.float32)],
            [live, parts, turned], "clip", 10000000000,
        )

    ps[1] = after(ps[1], part)
    advance(2)
    parts = lax.all_to_all(part, PLANE, 0, 0, tiled=False)
    block, norm = clipped(parts)
    advance(3)
    block = lax.ppermute(block, ALL, spread_pairs())
    advance(4)
    advance(5)
    [spread] = call(spread_kernel, [jax.ShapeDtypeStruct((NT, CHIP, SEQ), jnp.bfloat16)], [block], "spread", 10000000000)
    s = lax.all_to_all(spread, PLANE, 0, 0, tiled=False)
    advance(6)
    ps[6] = after(ps[6], cost=1000000000)
    advance(7)
    [acc] = matmul(s, range(0, 6), ps, qs, None)

    advance(8)
    [acc] = matmul(s, range(6, 8), ps, qs, acc)
    mine, theirs = matmul(s, range(8, 9), ps, qs, acc, core.astype(jnp.int32).reshape(1))
    total = mine + lax.ppermute(theirs, "core", SWAP)
    grad = (total / math.sqrt(NZ * NC * SEQ)).T
    return grad, norm[0, 0:1]


def solution(mesh):
    grid = Mesh(mesh.devices.reshape(NZ, NC, NY, NX), ALL)
    return jax.shard_map(
        per_device,
        mesh=grid,
        in_specs=(P(LINE, PLANE), P(LINE, None), P(LINE)),
        out_specs=(P(PLANE, LINE), P(LINE)),
        check_vma=False,
    )
```

```python
import math

import jax
import jax.numpy as jnp
from jax import lax
from jax.experimental import pallas as pl
from jax.experimental.pallas import tpu as pltpu
from jax.sharding import Mesh, PartitionSpec as P

D = 4608
UNITS = 18432
SEQ = 128
NZ, NC, NY, NX = 16, 2, 4, 4
NT = NY * NX
CHIP = D // NZ
OWN = CHIP // NC
HOPS = NZ // 2

LINE = ("z", "core")
PLANE = ("y", "x")
ALL = ("z", "core", "y", "x")
STEP = [(z * 2, (z + 1) % NZ * 2) for z in range(NZ)]
STEP += [(z * 2 + 1, (z - 1) % NZ * 2 + 1) for z in range(NZ)]
SWAP = [(0, 1), (1, 0)]


def spread_pairs():
    pairs = []
    for z in range(NZ):
        for c in range(NC):
            for t in range(NT):
                to_z = (z + t if c == 0 else z - t) % NZ
                to_c = c if t <= HOPS else 1 - c
                pairs.append(((z * NC + c) * NT + t, (to_z * NC + to_c) * NT + t))
    return pairs


def vmem():
    return pl.BlockSpec(memory_space=pltpu.VMEM)


def smem():
    return pl.BlockSpec(memory_space=pltpu.SMEM)


def call(kernel, outs, ins, name, flops, scratch=(), far=False, tokens=()):
    moved = sum(math.prod(a.shape) * a.dtype.itemsize for a in list(ins) + list(outs))
    if tokens:
        inner, n = kernel, len(ins)

        def kernel(*refs):
            inner(*refs[:n], *refs[n + len(tokens):])

    return pl.pallas_call(
        kernel,
        out_shape=outs,
        in_specs=[smem() if a.dtype == jnp.int32 else pl.BlockSpec(memory_space=pl.ANY) if far else vmem() for a in ins]
        + [pl.BlockSpec(memory_space=pl.ANY) for _ in tokens],
        out_specs=[vmem() for _ in outs],
        scratch_shapes=list(scratch),
        compiler_params=pltpu.CompilerParams(vmem_limit_bytes=16 * 1024 * 1024),
        cost_estimate=pl.CostEstimate(flops=flops, bytes_accessed=moved, transcendentals=0),
        name=name,
    )(*ins, *tokens)


def after(x, *others, cost=0):
    def kernel(*refs):
        del refs

    return pl.pallas_call(
        kernel,
        out_shape=jax.ShapeDtypeStruct(x.shape, x.dtype),
        in_specs=[pl.BlockSpec(memory_space=pl.ANY)] * (1 + len(others)),
        out_specs=pl.BlockSpec(memory_space=pl.ANY),
        input_output_aliases={0: 0},
        compiler_params=pltpu.CompilerParams(vmem_limit_bytes=1024 * 1024),
        cost_estimate=pl.CostEstimate(flops=cost, bytes_accessed=0, transcendentals=0),
        name="after",
    )(x, *others)


def gram_kernel(to_ref, h_hbm, g_hbm, part_ref, turned_ref, h_ref, g_ref, turned, h_sem, g_sem):
    h_copy = pltpu.make_async_copy(h_hbm, h_ref, h_sem)
    g_copy = pltpu.make_async_copy(g_hbm, g_ref, g_sem)
    h_copy.start()
    g_copy.start()
    dims = (((1,), (1,)), ((), ()))
    h_copy.wait()
    gram_h = lax.dot_general(h_ref[...], h_ref[...], dims, preferred_element_type=jnp.float32)
    g_copy.wait()
    gram_g = lax.dot_general(g_ref[...], g_ref[...], dims, preferred_element_type=jnp.float32)
    part_ref[...] = jnp.full(part_ref.shape, jnp.sum(gram_h * gram_g), jnp.float32)
    start = to_ref[0] * CHIP
    base = pl.multiple_of(start // 128 * 128, 128)
    turned[...] = g_ref[:, pl.ds(base, 384)].astype(jnp.float32).T
    turned_ref[...] = turned[pl.ds(pl.multiple_of(start - base, 32), CHIP), :]


def clip_kernel(live_ref, parts_ref, turned_ref, block_ref, norm_ref):
    total = jnp.sum(parts_ref[...], axis=0)[0:1, :]
    q = total / (float(SEQ) * float(UNITS) * float(D))
    live = live_ref[0].astype(jnp.float32)
    clip = live * jnp.minimum(1.0, 1.0 / jnp.sqrt(q + 1e-06))
    norm_ref[...] = jnp.broadcast_to(jnp.sqrt(q), norm_ref.shape)
    block_ref[...] = (turned_ref[...] * clip).astype(jnp.bfloat16)


def spread_kernel(block_ref, out_ref):
    block = block_ref[...]
    for t in range(NT):
        out_ref[t] = block


def matmul(s, pairs, acc, cost=0):
    blocks = [block for pair in pairs for block, _ in pair]
    ins = [s] + blocks + ([acc] if acc is not None else [])
    units = blocks[0].shape[1]

    def kernel(*refs):
        s_ref, rest = refs[0], list(refs[1:])
        taken = [[(rest.pop(0), at) for _, at in pair] for pair in pairs]
        total = rest.pop(0)[...] if acc is not None else None
        for pair in taken:
            if len(pair) == 1:
                [(p_ref, at)] = pair
                left, right = s_ref[at], p_ref[...]
            else:
                (p_ref, p_at), (q_ref, q_at) = pair
                left = jnp.concatenate([s_ref[p_at], s_ref[q_at]], axis=1)
                right = jnp.concatenate([p_ref[...], q_ref[...]], axis=0)
            term = jnp.dot(left, right, preferred_element_type=jnp.float32)
            total = term if total is None else total + term
        rest[0][...] = total

    flops = cost or 2 * CHIP * units * SEQ * len(blocks)
    return call(kernel, [jax.ShapeDtypeStruct((CHIP, units), jnp.float32)], ins, "products", flops)[0]


def last_products(rows, s, pair, acc, cost=0):
    units = acc.shape[1]

    def kernel(rows_ref, s_ref, *refs):
        blocks, acc_ref, out_ref = refs[:-2], refs[-2], refs[-1]
        at = rows_ref[0] * OWN
        own = pl.ds(pl.multiple_of(at, 16), OWN)
        left = [s_ref[place, own, :] for _, place in pair]
        right = [block[...] for block in blocks]
        left, right = [x[0] if len(x) == 1 else jnp.concatenate(x, axis=axis) for x, axis in ((left, 1), (right, 0))]
        out_ref[...] = acc_ref[pl.ds(pl.multiple_of(at, 8), OWN), :] + jnp.dot(left, right, preferred_element_type=jnp.float32)

    flops = cost or 2 * OWN * units * SEQ * len(pair)
    ins = [rows, s] + [block for block, _ in pair] + [acc]
    return call(kernel, [jax.ShapeDtypeStruct((OWN, units), jnp.float32)], ins, "last", flops)[0]


def per_device(hidden, out_grad, live):
    z, core = lax.axis_index("z"), lax.axis_index("core")
    t = lax.axis_index(PLANE)
    units = hidden.shape[1]

    ps, qs = [hidden], [None]
    own_q = lax.ppermute(hidden, "core", SWAP)

    def advance(hop):
        if hop < HOPS:
            qs.append(lax.ppermute(qs[-1] if hop > 1 else own_q, LINE, STEP))
        else:
            qs.append(None)
        ps.append(lax.ppermute(ps[-1], LINE, STEP))

    advance(1)

    to = lax.rem(z + (1 - 2 * core) * t + NZ, NZ).astype(jnp.int32).reshape(1)
    part, turned = call(
        gram_kernel,
        [jax.ShapeDtypeStruct((NT, 8, 128), jnp.float32), jax.ShapeDtypeStruct((CHIP, SEQ), jnp.float32)],
        [to, hidden, out_grad], "grams", 2 * SEQ * SEQ * (units + D),
        scratch=[pltpu.VMEM(hidden.shape, hidden.dtype), pltpu.VMEM(out_grad.shape, out_grad.dtype),
                 pltpu.VMEM((384, SEQ), jnp.float32), pltpu.SemaphoreType.DMA, pltpu.SemaphoreType.DMA],
        far=True,
    )
    def clipped(parts):
        return call(
            clip_kernel,
            [jax.ShapeDtypeStruct((CHIP, SEQ), jnp.bfloat16), jax.ShapeDtypeStruct((8, 128), jnp.float32)],
            [live, parts, turned], "clip", 10000000000,
        )

    ps[1] = after(ps[1], part)
    advance(2)
    parts = lax.all_to_all(part, PLANE, 0, 0, tiled=False)
    block, norm = clipped(parts)
    advance(3)
    block = lax.ppermute(block, ALL, spread_pairs())
    advance(4)
    advance(5)
    [spread] = call(spread_kernel, [jax.ShapeDtypeStruct((NT, CHIP, SEQ), jnp.bfloat16)], [block], "spread", 10000000000)
    s = lax.all_to_all(spread, PLANE, 0, 0, tiled=False)
    advance(6)
    qs[6] = after(qs[6], cost=4000000000)
    advance(7)
    advance(8)

    def pair(hop):
        return (ps[hop], hop), (qs[hop], NZ - hop)

    acc = matmul(s, [((ps[0], 0),)] + [pair(hop) for hop in range(1, 6)], None)
    acc = matmul(s, [pair(6), pair(7)], acc, 0)
    last = [(ps[HOPS], HOPS)]
    row = core.astype(jnp.int32).reshape(1)
    theirs = lax.ppermute(last_products(1 - row, s, last, acc, 0), "core", SWAP)
    total = last_products(row, s, last, acc) + theirs
    grad = (total / math.sqrt(NZ * NC * SEQ)).T
    return grad, norm[0, 0:1]


def solution(mesh):
    grid = Mesh(mesh.devices.reshape(NZ, NC, NY, NX), ALL)
    return jax.shard_map(
        per_device,
        mesh=grid,
        in_specs=(P(LINE, PLANE), P(LINE, None), P(LINE)),
        out_specs=(P(PLANE, LINE), P(LINE)),
        check_vma=False,
    )
```

```python
import math

import jax
import jax.numpy as jnp
from jax import lax
from jax.experimental import pallas as pl
from jax.experimental.pallas import tpu as pltpu
from jax.sharding import Mesh, PartitionSpec as P

D = 4608
UNITS = 18432
SEQ = 128
NZ, NC, NY, NX = 16, 2, 4, 4
NT = NY * NX
CHIP = D // NZ
OWN = CHIP // NC
HOPS = NZ // 2

LINE = ("z", "core")
PLANE = ("y", "x")
ALL = ("z", "core", "y", "x")
JUMP = 4


def step_pairs(steps):
    return [(z * 2, (z + steps) % NZ * 2) for z in range(NZ)] + [(z * 2 + 1, (z - steps) % NZ * 2 + 1) for z in range(NZ)]


SWAP = [(0, 1), (1, 0)]


def spread_pairs():
    pairs = []
    for z in range(NZ):
        for c in range(NC):
            for t in range(NT):
                to_z = (z + t if c == 0 else z - t) % NZ
                to_c = c if t <= HOPS else 1 - c
                pairs.append(((z * NC + c) * NT + t, (to_z * NC + to_c) * NT + t))
    return pairs


def vmem():
    return pl.BlockSpec(memory_space=pltpu.VMEM)


def smem():
    return pl.BlockSpec(memory_space=pltpu.SMEM)


def call(kernel, outs, ins, name, flops, scratch=(), far=False, tokens=()):
    moved = sum(math.prod(a.shape) * a.dtype.itemsize for a in list(ins) + list(outs))
    if tokens:
        inner, n = kernel, len(ins)

        def kernel(*refs):
            inner(*refs[:n], *refs[n + len(tokens):])

    return pl.pallas_call(
        kernel,
        out_shape=outs,
        in_specs=[smem() if a.dtype == jnp.int32 else pl.BlockSpec(memory_space=pl.ANY) if far else vmem() for a in ins]
        + [pl.BlockSpec(memory_space=pl.ANY) for _ in tokens],
        out_specs=[vmem() for _ in outs],
        scratch_shapes=list(scratch),
        compiler_params=pltpu.CompilerParams(vmem_limit_bytes=16 * 1024 * 1024),
        cost_estimate=pl.CostEstimate(flops=flops, bytes_accessed=moved, transcendentals=0),
        name=name,
    )(*ins, *tokens)


def after(x, *others, cost=0):
    def kernel(*refs):
        del refs

    return pl.pallas_call(
        kernel,
        out_shape=jax.ShapeDtypeStruct(x.shape, x.dtype),
        in_specs=[pl.BlockSpec(memory_space=pl.ANY)] * (1 + len(others)),
        out_specs=pl.BlockSpec(memory_space=pl.ANY),
        input_output_aliases={0: 0},
        compiler_params=pltpu.CompilerParams(vmem_limit_bytes=1024 * 1024),
        cost_estimate=pl.CostEstimate(flops=cost, bytes_accessed=0, transcendentals=0),
        name="after",
    )(x, *others)


def gram_kernel(to_ref, h_hbm, g_hbm, part_ref, turned_ref, h_ref, g_ref, turned, h_sem, g_sem):
    h_copy = pltpu.make_async_copy(h_hbm, h_ref, h_sem)
    g_copy = pltpu.make_async_copy(g_hbm, g_ref, g_sem)
    h_copy.start()
    g_copy.start()
    dims = (((1,), (1,)), ((), ()))
    h_copy.wait()
    gram_h = lax.dot_general(h_ref[...], h_ref[...], dims, preferred_element_type=jnp.float32)
    g_copy.wait()
    gram_g = lax.dot_general(g_ref[...], g_ref[...], dims, preferred_element_type=jnp.float32)
    part_ref[...] = jnp.full(part_ref.shape, jnp.sum(gram_h * gram_g), jnp.float32)
    start = to_ref[0] * CHIP
    base = pl.multiple_of(start // 128 * 128, 128)
    turned[...] = g_ref[:, pl.ds(base, 384)].astype(jnp.float32).T
    turned_ref[...] = turned[pl.ds(pl.multiple_of(start - base, 32), CHIP), :]


def clip_kernel(live_ref, parts_ref, turned_ref, block_ref, norm_ref):
    total = jnp.sum(parts_ref[...], axis=0)[0:1, :]
    q = total / (float(SEQ) * float(UNITS) * float(D))
    live = live_ref[0].astype(jnp.float32)
    clip = live * jnp.minimum(1.0, 1.0 / jnp.sqrt(q + 1e-06))
    norm_ref[...] = jnp.broadcast_to(jnp.sqrt(q), norm_ref.shape)
    block_ref[...] = (turned_ref[...] * clip).astype(jnp.bfloat16)


def spread_kernel(block_ref, out_ref):
    block = block_ref[...]
    for t in range(NT):
        out_ref[t] = block


def matmul(s, blocks, hops, acc, cost=0):
    given = [blocks[hop] if isinstance(blocks[hop], tuple) else (blocks[hop],) for hop in hops]
    ins = [s] + [part for block in given for part in block] + ([acc] if acc is not None else [])
    units = given[0][0].shape[1]

    def kernel(*refs):
        s_ref, rest = refs[0], list(refs[1:])
        taken = [[rest.pop(0) for _ in block] for block in given]
        total = rest.pop(0)[...] if acc is not None else None
        for hop, parts in zip(hops, taken):
            right = parts[0][...] if len(parts) == 1 else jnp.concatenate([part[...] for part in parts], axis=0)
            left = s_ref[hop]
            if right.shape[0] > SEQ:
                left = jnp.concatenate([left, s_ref[NZ - hop]], axis=1)
            term = jnp.dot(left, right, preferred_element_type=jnp.float32)
            total = term if total is None else total + term
        rest[0][...] = total

    flops = cost or 4 * CHIP * units * SEQ * len(hops)
    return call(kernel, [jax.ShapeDtypeStruct((CHIP, units), jnp.float32)], ins, "products", flops)[0]


def last_products(rows, s, pair, acc, cost=0):
    units = acc.shape[1]

    def kernel(rows_ref, s_ref, *refs):
        blocks, acc_ref, out_ref = refs[:-2], refs[-2], refs[-1]
        at = rows_ref[0] * OWN
        own = pl.ds(pl.multiple_of(at, 16), OWN)
        left = [s_ref[place, own, :] for _, place in pair]
        right = [block[...] for block in blocks]
        left, right = [x[0] if len(x) == 1 else jnp.concatenate(x, axis=axis) for x, axis in ((left, 1), (right, 0))]
        out_ref[...] = acc_ref[pl.ds(pl.multiple_of(at, 8), OWN), :] + jnp.dot(left, right, preferred_element_type=jnp.float32)

    flops = cost or 2 * OWN * units * SEQ * len(pair)
    ins = [rows, s] + [block for block, _ in pair] + [acc]
    return call(kernel, [jax.ShapeDtypeStruct((OWN, units), jnp.float32)], ins, "last", flops)[0]


def per_device(hidden, out_grad, live):
    z, core = lax.axis_index("z"), lax.axis_index("core")
    t = lax.axis_index(PLANE)
    units = hidden.shape[1]

    both = jnp.concatenate([hidden, lax.ppermute(hidden, "core", SWAP)], axis=0)
    blocks = {0: hidden, JUMP: lax.ppermute(both, LINE, step_pairs(JUMP))}
    blocks[1] = lax.ppermute(both, LINE, step_pairs(1))
    for hop in range(2, 7):
        if hop != JUMP:
            blocks[hop] = lax.ppermute(blocks[hop - 1], LINE, step_pairs(1))
    p, q = blocks[6][:SEQ], blocks[6][SEQ:]
    for hop in range(7, HOPS + 1):
        p = lax.ppermute(p, LINE, step_pairs(1))
        q = lax.ppermute(q, LINE, step_pairs(1)) if hop < HOPS else None
        blocks[hop] = (p, q)

    to = lax.rem(z + (1 - 2 * core) * t + NZ, NZ).astype(jnp.int32).reshape(1)
    part, turned = call(
        gram_kernel,
        [jax.ShapeDtypeStruct((NT, 8, 128), jnp.float32), jax.ShapeDtypeStruct((CHIP, SEQ), jnp.float32)],
        [to, hidden, out_grad], "grams", 2 * SEQ * SEQ * (units + D),
        scratch=[pltpu.VMEM(hidden.shape, hidden.dtype), pltpu.VMEM(out_grad.shape, out_grad.dtype),
                 pltpu.VMEM((384, SEQ), jnp.float32), pltpu.SemaphoreType.DMA, pltpu.SemaphoreType.DMA],
        far=True,
    )
    def clipped(parts):
        return call(
            clip_kernel,
            [jax.ShapeDtypeStruct((CHIP, SEQ), jnp.bfloat16), jax.ShapeDtypeStruct((8, 128), jnp.float32)],
            [live, parts, turned], "clip", 10000000000,
        )

    parts = lax.all_to_all(part, PLANE, 0, 0, tiled=False)
    block, norm = clipped(parts)
    block = lax.ppermute(block, ALL, spread_pairs())
    [spread] = call(spread_kernel, [jax.ShapeDtypeStruct((NT, CHIP, SEQ), jnp.bfloat16)], [block], "spread", 10000000000)
    s = lax.all_to_all(spread, PLANE, 0, 0, tiled=False)

    acc = matmul(s, blocks, range(0, 7), None)
    acc = matmul(s, blocks, range(7, HOPS), acc, 0)
    last = [(blocks[HOPS][0], HOPS)]
    row = core.astype(jnp.int32).reshape(1)
    theirs = lax.ppermute(last_products(1 - row, s, last, acc, 0), "core", SWAP)
    total = last_products(row, s, last, acc) + theirs
    grad = (total / math.sqrt(NZ * NC * SEQ)).T
    return grad, norm[0, 0:1]


def solution(mesh):
    grid = Mesh(mesh.devices.reshape(NZ, NC, NY, NX), ALL)
    return jax.shard_map(
        per_device,
        mesh=grid,
        in_specs=(P(LINE, PLANE), P(LINE, None), P(LINE)),
        out_specs=(P(PLANE, LINE), P(LINE)),
        check_vma=False,
    )
```

```python
import math

import jax
import jax.numpy as jnp
from jax import lax
from jax.experimental import pallas as pl
from jax.experimental.pallas import tpu as pltpu
from jax.sharding import Mesh, PartitionSpec as P

D = 4608
UNITS = 18432
SEQ = 128
NZ, NC, NY, NX = 16, 2, 4, 4
NT = NY * NX
CHIP = D // NZ
OWN = CHIP // NC
HOPS = NZ // 2

LINE = ("z", "core")
PLANE = ("y", "x")
ALL = ("z", "core", "y", "x")
JUMP = 3


def step_pairs(steps):
    return [(z * 2, (z + steps) % NZ * 2) for z in range(NZ)] + [(z * 2 + 1, (z - steps) % NZ * 2 + 1) for z in range(NZ)]


SWAP = [(0, 1), (1, 0)]


def spread_pairs():
    pairs = []
    for z in range(NZ):
        for c in range(NC):
            for t in range(NT):
                to_z = (z + t if c == 0 else z - t) % NZ
                to_c = c if t <= HOPS else 1 - c
                pairs.append(((z * NC + c) * NT + t, (to_z * NC + to_c) * NT + t))
    return pairs


def vmem():
    return pl.BlockSpec(memory_space=pltpu.VMEM)


def smem():
    return pl.BlockSpec(memory_space=pltpu.SMEM)


def call(kernel, outs, ins, name, flops, scratch=(), far=False, tokens=()):
    moved = sum(math.prod(a.shape) * a.dtype.itemsize for a in list(ins) + list(outs))
    if tokens:
        inner, n = kernel, len(ins)

        def kernel(*refs):
            inner(*refs[:n], *refs[n + len(tokens):])

    return pl.pallas_call(
        kernel,
        out_shape=outs,
        in_specs=[smem() if a.dtype == jnp.int32 else pl.BlockSpec(memory_space=pl.ANY) if far else vmem() for a in ins]
        + [pl.BlockSpec(memory_space=pl.ANY) for _ in tokens],
        out_specs=[vmem() for _ in outs],
        scratch_shapes=list(scratch),
        compiler_params=pltpu.CompilerParams(vmem_limit_bytes=16 * 1024 * 1024),
        cost_estimate=pl.CostEstimate(flops=flops, bytes_accessed=moved, transcendentals=0),
        name=name,
    )(*ins, *tokens)


def after(x, *others, cost=0):
    def kernel(*refs):
        del refs

    return pl.pallas_call(
        kernel,
        out_shape=jax.ShapeDtypeStruct(x.shape, x.dtype),
        in_specs=[pl.BlockSpec(memory_space=pl.ANY)] * (1 + len(others)),
        out_specs=pl.BlockSpec(memory_space=pl.ANY),
        input_output_aliases={0: 0},
        compiler_params=pltpu.CompilerParams(vmem_limit_bytes=1024 * 1024),
        cost_estimate=pl.CostEstimate(flops=cost, bytes_accessed=0, transcendentals=0),
        name="after",
    )(x, *others)


def gram_kernel(to_ref, h_hbm, g_hbm, part_ref, turned_ref, h_ref, g_ref, turned, h_sem, g_sem):
    h_copy = pltpu.make_async_copy(h_hbm, h_ref, h_sem)
    g_copy = pltpu.make_async_copy(g_hbm, g_ref, g_sem)
    h_copy.start()
    g_copy.start()
    dims = (((1,), (1,)), ((), ()))
    h_copy.wait()
    gram_h = lax.dot_general(h_ref[...], h_ref[...], dims, preferred_element_type=jnp.float32)
    g_copy.wait()
    gram_g = lax.dot_general(g_ref[...], g_ref[...], dims, preferred_element_type=jnp.float32)
    part_ref[...] = jnp.full(part_ref.shape, jnp.sum(gram_h * gram_g), jnp.float32)
    start = to_ref[0] * CHIP
    base = pl.multiple_of(start // 128 * 128, 128)
    turned[...] = g_ref[:, pl.ds(base, 384)].astype(jnp.float32).T
    turned_ref[...] = turned[pl.ds(pl.multiple_of(start - base, 32), CHIP), :]


def clip_kernel(live_ref, parts_ref, turned_ref, block_ref, norm_ref):
    total = jnp.sum(parts_ref[...], axis=0)[0:1, :]
    q = total / (float(SEQ) * float(UNITS) * float(D))
    live = live_ref[0].astype(jnp.float32)
    clip = live * jnp.minimum(1.0, 1.0 / jnp.sqrt(q + 1e-06))
    norm_ref[...] = jnp.broadcast_to(jnp.sqrt(q), norm_ref.shape)
    block_ref[...] = (turned_ref[...] * clip).astype(jnp.bfloat16)


def spread_kernel(block_ref, out_ref):
    block = block_ref[...]
    for t in range(NT):
        out_ref[t] = block


def matmul(s, blocks, hops, acc, cost=0):
    given = [blocks[hop] if isinstance(blocks[hop], tuple) else (blocks[hop],) for hop in hops]
    ins = [s] + [part for block in given for part in block] + ([acc] if acc is not None else [])
    units = given[0][0].shape[1]

    def kernel(*refs):
        s_ref, rest = refs[0], list(refs[1:])
        taken = [[rest.pop(0) for _ in block] for block in given]
        total = rest.pop(0)[...] if acc is not None else None
        for hop, parts in zip(hops, taken):
            right = parts[0][...] if len(parts) == 1 else jnp.concatenate([part[...] for part in parts], axis=0)
            left = s_ref[hop]
            if right.shape[0] > SEQ:
                left = jnp.concatenate([left, s_ref[NZ - hop]], axis=1)
            term = jnp.dot(left, right, preferred_element_type=jnp.float32)
            total = term if total is None else total + term
        rest[0][...] = total

    flops = cost or 4 * CHIP * units * SEQ * len(hops)
    return call(kernel, [jax.ShapeDtypeStruct((CHIP, units), jnp.float32)], ins, "products", flops)[0]


def last_products(rows, s, pair, acc, cost=0):
    units = acc.shape[1]

    def kernel(rows_ref, s_ref, *refs):
        blocks, acc_ref, out_ref = refs[:-2], refs[-2], refs[-1]
        at = rows_ref[0] * OWN
        own = pl.ds(pl.multiple_of(at, 16), OWN)
        left = [s_ref[place, own, :] for _, place in pair]
        right = [block[...] for block in blocks]
        left, right = [x[0] if len(x) == 1 else jnp.concatenate(x, axis=axis) for x, axis in ((left, 1), (right, 0))]
        out_ref[...] = acc_ref[pl.ds(pl.multiple_of(at, 8), OWN), :] + jnp.dot(left, right, preferred_element_type=jnp.float32)

    flops = cost or 2 * OWN * units * SEQ * len(pair)
    ins = [rows, s] + [block for block, _ in pair] + [acc]
    return call(kernel, [jax.ShapeDtypeStruct((OWN, units), jnp.float32)], ins, "last", flops)[0]


def per_device(hidden, out_grad, live):
    z, core = lax.axis_index("z"), lax.axis_index("core")
    t = lax.axis_index(PLANE)
    units = hidden.shape[1]

    other = lax.ppermute(hidden, "core", SWAP)
    both = jnp.concatenate([hidden, other], axis=0)
    blocks = {0: hidden}
    for hop in range(1, JUMP):
        blocks[hop] = lax.ppermute(blocks[hop - 1] if hop > 1 else both, LINE, step_pairs(1))

    p, q = lax.ppermute(hidden, LINE, step_pairs(JUMP)), lax.ppermute(other, LINE, step_pairs(JUMP))
    blocks[JUMP] = (p, q)
    for hop in range(JUMP + 1, HOPS + 1):
        p = lax.ppermute(p, LINE, step_pairs(1))
        q = lax.ppermute(q, LINE, step_pairs(1)) if hop < HOPS else None
        if hop == 6:
            p = after(p, cost=2000000000)
        if hop == 6:
            q = after(q, cost=4000000000)
        blocks[hop] = (p, q)

    to = lax.rem(z + (1 - 2 * core) * t + NZ, NZ).astype(jnp.int32).reshape(1)
    part, turned = call(
        gram_kernel,
        [jax.ShapeDtypeStruct((NT, 8, 128), jnp.float32), jax.ShapeDtypeStruct((CHIP, SEQ), jnp.float32)],
        [to, hidden, out_grad], "grams", 2 * SEQ * SEQ * (units + D),
        scratch=[pltpu.VMEM(hidden.shape, hidden.dtype), pltpu.VMEM(out_grad.shape, out_grad.dtype),
                 pltpu.VMEM((384, SEQ), jnp.float32), pltpu.SemaphoreType.DMA, pltpu.SemaphoreType.DMA],
        far=True,
    )
    def clipped(parts):
        return call(
            clip_kernel,
            [jax.ShapeDtypeStruct((CHIP, SEQ), jnp.bfloat16), jax.ShapeDtypeStruct((8, 128), jnp.float32)],
            [live, parts, turned], "clip", 10000000000,
        )

    parts = lax.all_to_all(part, PLANE, 0, 0, tiled=False)
    block, norm = clipped(parts)
    block = lax.ppermute(block, ALL, spread_pairs())
    [spread] = call(spread_kernel, [jax.ShapeDtypeStruct((NT, CHIP, SEQ), jnp.bfloat16)], [block], "spread", 10000000000)
    s = lax.all_to_all(spread, PLANE, 0, 0, tiled=False)

    acc = matmul(s, blocks, range(0, 4), None)
    acc = matmul(s, blocks, range(4, HOPS), acc, 0)
    last = [(blocks[HOPS][0], HOPS)]
    row = core.astype(jnp.int32).reshape(1)
    theirs = lax.ppermute(last_products(1 - row, s, last, acc, 0), "core", SWAP)
    total = last_products(row, s, last, acc) + theirs
    grad = (total / math.sqrt(NZ * NC * SEQ)).T
    return grad, norm[0, 0:1]


def solution(mesh):
    grid = Mesh(mesh.devices.reshape(NZ, NC, NY, NX), ALL)
    return jax.shard_map(
        per_device,
        mesh=grid,
        in_specs=(P(LINE, PLANE), P(LINE, None), P(LINE)),
        out_specs=(P(PLANE, LINE), P(LINE)),
        check_vma=False,
    )
```

```python
import math

import jax
import jax.numpy as jnp
from jax import lax
from jax.experimental import pallas as pl
from jax.experimental.pallas import tpu as pltpu
from jax.sharding import Mesh, PartitionSpec as P

D = 4608
UNITS = 18432
SEQ = 128
NZ, NC, NY, NX = 16, 2, 4, 4
NT = NY * NX
CHIP = D // NZ
OWN = CHIP // NC
HOPS = NZ // 2

LINE = ("z", "core")
PLANE = ("y", "x")
ALL = ("z", "core", "y", "x")
JUMP = 3


def step_pairs(steps):
    return [(z * 2, (z + steps) % NZ * 2) for z in range(NZ)] + [(z * 2 + 1, (z - steps) % NZ * 2 + 1) for z in range(NZ)]


SWAP = [(0, 1), (1, 0)]


def spread_pairs():
    pairs = []
    for z in range(NZ):
        for c in range(NC):
            for t in range(NT):
                to_z = (z + t if c == 0 else z - t) % NZ
                to_c = c if t <= HOPS else 1 - c
                pairs.append(((z * NC + c) * NT + t, (to_z * NC + to_c) * NT + t))
    return pairs


def vmem():
    return pl.BlockSpec(memory_space=pltpu.VMEM)


def smem():
    return pl.BlockSpec(memory_space=pltpu.SMEM)


def call(kernel, outs, ins, name, flops, scratch=(), far=False, tokens=()):
    moved = sum(math.prod(a.shape) * a.dtype.itemsize for a in list(ins) + list(outs))
    if tokens:
        inner, n = kernel, len(ins)

        def kernel(*refs):
            inner(*refs[:n], *refs[n + len(tokens):])

    return pl.pallas_call(
        kernel,
        out_shape=outs,
        in_specs=[smem() if a.dtype == jnp.int32 else pl.BlockSpec(memory_space=pl.ANY) if far else vmem() for a in ins]
        + [pl.BlockSpec(memory_space=pl.ANY) for _ in tokens],
        out_specs=[vmem() for _ in outs],
        scratch_shapes=list(scratch),
        compiler_params=pltpu.CompilerParams(vmem_limit_bytes=16 * 1024 * 1024),
        cost_estimate=pl.CostEstimate(flops=flops, bytes_accessed=moved, transcendentals=0),
        name=name,
    )(*ins, *tokens)


def after(x, *others, cost=0):
    def kernel(*refs):
        del refs

    return pl.pallas_call(
        kernel,
        out_shape=jax.ShapeDtypeStruct(x.shape, x.dtype),
        in_specs=[pl.BlockSpec(memory_space=pl.ANY)] * (1 + len(others)),
        out_specs=pl.BlockSpec(memory_space=pl.ANY),
        input_output_aliases={0: 0},
        compiler_params=pltpu.CompilerParams(vmem_limit_bytes=1024 * 1024),
        cost_estimate=pl.CostEstimate(flops=cost, bytes_accessed=0, transcendentals=0),
        name="after",
    )(x, *others)


def gram_kernel(to_ref, h_hbm, g_hbm, part_ref, turned_ref, h_ref, g_ref, turned, h_sem, g_sem):
    h_copy = pltpu.make_async_copy(h_hbm, h_ref, h_sem)
    g_copy = pltpu.make_async_copy(g_hbm, g_ref, g_sem)
    h_copy.start()
    g_copy.start()
    dims = (((1,), (1,)), ((), ()))
    h_copy.wait()
    gram_h = lax.dot_general(h_ref[...], h_ref[...], dims, preferred_element_type=jnp.float32)
    g_copy.wait()
    gram_g = lax.dot_general(g_ref[...], g_ref[...], dims, preferred_element_type=jnp.float32)
    part_ref[...] = jnp.full(part_ref.shape, jnp.sum(gram_h * gram_g), jnp.float32)
    start = to_ref[0] * CHIP
    base = pl.multiple_of(start // 128 * 128, 128)
    turned[...] = g_ref[:, pl.ds(base, 384)].astype(jnp.float32).T
    turned_ref[...] = turned[pl.ds(pl.multiple_of(start - base, 32), CHIP), :]


def clip_kernel(live_ref, parts_ref, turned_ref, block_ref, norm_ref):
    total = jnp.sum(parts_ref[...], axis=0)[0:1, :]
    q = total / (float(SEQ) * float(UNITS) * float(D))
    live = live_ref[0].astype(jnp.float32)
    clip = live * jnp.minimum(1.0, 1.0 / jnp.sqrt(q + 1e-06))
    norm_ref[...] = jnp.broadcast_to(jnp.sqrt(q), norm_ref.shape)
    block_ref[...] = (turned_ref[...] * clip).astype(jnp.bfloat16)


def spread_kernel(block_ref, out_ref):
    block = block_ref[...]
    for t in range(NT):
        out_ref[t] = block


def matmul(s, blocks, hops, acc, cost=0):
    given = [blocks[hop] if isinstance(blocks[hop], tuple) else (blocks[hop],) for hop in hops]
    ins = [s] + [part for block in given for part in block] + ([acc] if acc is not None else [])
    units = given[0][0].shape[1]

    def kernel(*refs):
        s_ref, rest = refs[0], list(refs[1:])
        taken = [[rest.pop(0) for _ in block] for block in given]
        total = rest.pop(0)[...] if acc is not None else None
        for hop, parts in zip(hops, taken):
            right = parts[0][...] if len(parts) == 1 else jnp.concatenate([part[...] for part in parts], axis=0)
            left = s_ref[hop]
            if right.shape[0] > SEQ:
                left = jnp.concatenate([left, s_ref[NZ - hop]], axis=1)
            term = jnp.dot(left, right, preferred_element_type=jnp.float32)
            total = term if total is None else total + term
        rest[0][...] = total

    flops = cost or 4 * CHIP * units * SEQ * len(hops)
    return call(kernel, [jax.ShapeDtypeStruct((CHIP, units), jnp.float32)], ins, "products", flops)[0]


def last_products(rows, s, pair, acc, cost=0):
    units = acc.shape[1]

    def kernel(rows_ref, s_ref, *refs):
        blocks, acc_ref, out_ref = refs[:-2], refs[-2], refs[-1]
        at = rows_ref[0] * OWN
        own = pl.ds(pl.multiple_of(at, 16), OWN)
        left = [s_ref[place, own, :] for _, place in pair]
        right = [block[...] for block in blocks]
        left, right = [x[0] if len(x) == 1 else jnp.concatenate(x, axis=axis) for x, axis in ((left, 1), (right, 0))]
        out_ref[...] = acc_ref[pl.ds(pl.multiple_of(at, 8), OWN), :] + jnp.dot(left, right, preferred_element_type=jnp.float32)

    flops = cost or 2 * OWN * units * SEQ * len(pair)
    ins = [rows, s] + [block for block, _ in pair] + [acc]
    return call(kernel, [jax.ShapeDtypeStruct((OWN, units), jnp.float32)], ins, "last", flops)[0]


def per_device(hidden, out_grad, live):
    z, core = lax.axis_index("z"), lax.axis_index("core")
    t = lax.axis_index(PLANE)
    units = hidden.shape[1]

    other = lax.ppermute(hidden, "core", SWAP)
    both = jnp.concatenate([hidden, other], axis=0)
    blocks = {0: hidden}
    for hop in range(1, JUMP):
        blocks[hop] = lax.ppermute(blocks[hop - 1] if hop > 1 else both, LINE, step_pairs(1))

    p, q = lax.ppermute(hidden, LINE, step_pairs(JUMP)), lax.ppermute(other, LINE, step_pairs(JUMP))
    blocks[JUMP] = (p, q)
    for hop in range(JUMP + 1, HOPS + 1):
        p = lax.ppermute(p, LINE, step_pairs(1))
        q = lax.ppermute(q, LINE, step_pairs(1)) if hop < HOPS else None
        if hop == 6:
            p, q = after(p, blocks[2], cost=2000000000), after(q, cost=4000000000)
        blocks[hop] = (p, q)

    to = lax.rem(z + (1 - 2 * core) * t + NZ, NZ).astype(jnp.int32).reshape(1)
    part, turned = call(
        gram_kernel,
        [jax.ShapeDtypeStruct((NT, 8, 128), jnp.float32), jax.ShapeDtypeStruct((CHIP, SEQ), jnp.float32)],
        [to, hidden, out_grad], "grams", 2 * SEQ * SEQ * (units + D),
        scratch=[pltpu.VMEM(hidden.shape, hidden.dtype), pltpu.VMEM(out_grad.shape, out_grad.dtype),
                 pltpu.VMEM((384, SEQ), jnp.float32), pltpu.SemaphoreType.DMA, pltpu.SemaphoreType.DMA],
        far=True,
    )
    def clipped(parts):
        return call(
            clip_kernel,
            [jax.ShapeDtypeStruct((CHIP, SEQ), jnp.bfloat16), jax.ShapeDtypeStruct((8, 128), jnp.float32)],
            [live, parts, turned], "clip", 10000000000,
        )

    parts = lax.all_to_all(part, PLANE, 0, 0, tiled=False)
    block, norm = clipped(parts)
    block = lax.ppermute(block, ALL, spread_pairs())
    [spread] = call(spread_kernel, [jax.ShapeDtypeStruct((NT, CHIP, SEQ), jnp.bfloat16)], [block], "spread", 10000000000)
    s = lax.all_to_all(spread, PLANE, 0, 0, tiled=False)

    acc = matmul(s, blocks, range(0, 4), None)
    acc = matmul(s, blocks, range(4, HOPS), acc, 0)
    last = [(blocks[HOPS][0], HOPS)]
    row = core.astype(jnp.int32).reshape(1)
    theirs = lax.ppermute(last_products(1 - row, s, last, acc, 0), "core", SWAP)
    total = last_products(row, s, last, acc) + theirs
    grad = (total / math.sqrt(NZ * NC * SEQ)).T
    return grad, norm[0, 0:1]


def solution(mesh):
    grid = Mesh(mesh.devices.reshape(NZ, NC, NY, NX), ALL)
    return jax.shard_map(
        per_device,
        mesh=grid,
        in_specs=(P(LINE, PLANE), P(LINE, None), P(LINE)),
        out_specs=(P(PLANE, LINE), P(LINE)),
        check_vma=False,
    )
```

```python
import math

import jax
import jax.numpy as jnp
from jax import lax
from jax.experimental import pallas as pl
from jax.experimental.pallas import tpu as pltpu
from jax.sharding import Mesh, PartitionSpec as P

D = 4608
UNITS = 18432
SEQ = 128
NZ, NC, NY, NX = 16, 2, 4, 4
NT = NY * NX
CHIP = D // NZ
OWN = CHIP // NC
HOPS = NZ // 2

LINE = ("z", "core")
PLANE = ("y", "x")
ALL = ("z", "core", "y", "x")
JUMP = 3


def step_pairs(steps):
    return [(z * 2, (z + steps) % NZ * 2) for z in range(NZ)] + [(z * 2 + 1, (z - steps) % NZ * 2 + 1) for z in range(NZ)]


SWAP = [(0, 1), (1, 0)]


def spread_pairs():
    pairs = []
    for z in range(NZ):
        for c in range(NC):
            for t in range(NT):
                to_z = (z + t if c == 0 else z - t) % NZ
                to_c = c if t <= HOPS else 1 - c
                pairs.append(((z * NC + c) * NT + t, (to_z * NC + to_c) * NT + t))
    return pairs


def vmem():
    return pl.BlockSpec(memory_space=pltpu.VMEM)


def smem():
    return pl.BlockSpec(memory_space=pltpu.SMEM)


def call(kernel, outs, ins, name, flops, scratch=(), far=False, tokens=()):
    moved = sum(math.prod(a.shape) * a.dtype.itemsize for a in list(ins) + list(outs))
    if tokens:
        inner, n = kernel, len(ins)

        def kernel(*refs):
            inner(*refs[:n], *refs[n + len(tokens):])

    return pl.pallas_call(
        kernel,
        out_shape=outs,
        in_specs=[smem() if a.dtype == jnp.int32 else pl.BlockSpec(memory_space=pl.ANY) if far else vmem() for a in ins]
        + [pl.BlockSpec(memory_space=pl.ANY) for _ in tokens],
        out_specs=[vmem() for _ in outs],
        scratch_shapes=list(scratch),
        compiler_params=pltpu.CompilerParams(vmem_limit_bytes=16 * 1024 * 1024),
        cost_estimate=pl.CostEstimate(flops=flops, bytes_accessed=moved, transcendentals=0),
        name=name,
    )(*ins, *tokens)


def after(x, *others, cost=0):
    def kernel(*refs):
        del refs

    return pl.pallas_call(
        kernel,
        out_shape=jax.ShapeDtypeStruct(x.shape, x.dtype),
        in_specs=[pl.BlockSpec(memory_space=pl.ANY)] * (1 + len(others)),
        out_specs=pl.BlockSpec(memory_space=pl.ANY),
        input_output_aliases={0: 0},
        compiler_params=pltpu.CompilerParams(vmem_limit_bytes=1024 * 1024),
        cost_estimate=pl.CostEstimate(flops=cost, bytes_accessed=0, transcendentals=0),
        name="after",
    )(x, *others)


def gram_kernel(to_ref, h_hbm, g_hbm, part_ref, turned_ref, h_ref, g_ref, turned, h_sem, g_sem):
    h_copy = pltpu.make_async_copy(h_hbm, h_ref, h_sem)
    g_copy = pltpu.make_async_copy(g_hbm, g_ref, g_sem)
    h_copy.start()
    g_copy.start()
    dims = (((1,), (1,)), ((), ()))
    h_copy.wait()
    gram_h = lax.dot_general(h_ref[...], h_ref[...], dims, preferred_element_type=jnp.float32)
    g_copy.wait()
    gram_g = lax.dot_general(g_ref[...], g_ref[...], dims, preferred_element_type=jnp.float32)
    part_ref[...] = jnp.full(part_ref.shape, jnp.sum(gram_h * gram_g), jnp.float32)
    start = to_ref[0] * CHIP
    base = pl.multiple_of(start // 128 * 128, 128)
    turned[...] = g_ref[:, pl.ds(base, 384)].astype(jnp.float32).T
    turned_ref[...] = turned[pl.ds(pl.multiple_of(start - base, 32), CHIP), :]


def clip_kernel(live_ref, parts_ref, turned_ref, block_ref, norm_ref):
    total = jnp.sum(parts_ref[...], axis=0)[0:1, :]
    q = total / (float(SEQ) * float(UNITS) * float(D))
    live = live_ref[0].astype(jnp.float32)
    clip = live * jnp.minimum(1.0, 1.0 / jnp.sqrt(q + 1e-06))
    norm_ref[...] = jnp.broadcast_to(jnp.sqrt(q), norm_ref.shape)
    block_ref[...] = (turned_ref[...] * clip).astype(jnp.bfloat16)


def spread_kernel(block_ref, out_ref):
    block = block_ref[...]
    for t in range(NT):
        out_ref[t] = block


def matmul(s, blocks, hops, acc, cost=0):
    given = [blocks[hop] if isinstance(blocks[hop], tuple) else (blocks[hop],) for hop in hops]
    ins = [s] + [part for block in given for part in block] + ([acc] if acc is not None else [])
    units = given[0][0].shape[1]

    def kernel(*refs):
        s_ref, rest = refs[0], list(refs[1:])
        taken = [[rest.pop(0) for _ in block] for block in given]
        total = rest.pop(0)[...] if acc is not None else None
        for hop, parts in zip(hops, taken):
            right = parts[0][...] if len(parts) == 1 else jnp.concatenate([part[...] for part in parts], axis=0)
            left = s_ref[hop]
            if right.shape[0] > SEQ:
                left = jnp.concatenate([left, s_ref[NZ - hop]], axis=1)
            term = jnp.dot(left, right, preferred_element_type=jnp.float32)
            total = term if total is None else total + term
        rest[0][...] = total

    flops = cost or 4 * CHIP * units * SEQ * len(hops)
    return call(kernel, [jax.ShapeDtypeStruct((CHIP, units), jnp.float32)], ins, "products", flops)[0]


def last_products(rows, s, pair, acc, cost=0):
    units = acc.shape[1]

    def kernel(rows_ref, s_ref, *refs):
        blocks, acc_ref, out_ref = refs[:-2], refs[-2], refs[-1]
        at = rows_ref[0] * OWN
        own = pl.ds(pl.multiple_of(at, 16), OWN)
        left = [s_ref[place, own, :] for _, place in pair]
        right = [block[...] for block in blocks]
        left, right = [x[0] if len(x) == 1 else jnp.concatenate(x, axis=axis) for x, axis in ((left, 1), (right, 0))]
        out_ref[...] = acc_ref[pl.ds(pl.multiple_of(at, 8), OWN), :] + jnp.dot(left, right, preferred_element_type=jnp.float32)

    flops = cost or 2 * OWN * units * SEQ * len(pair)
    ins = [rows, s] + [block for block, _ in pair] + [acc]
    return call(kernel, [jax.ShapeDtypeStruct((OWN, units), jnp.float32)], ins, "last", flops)[0]


def per_device(hidden, out_grad, live):
    z, core = lax.axis_index("z"), lax.axis_index("core")
    t = lax.axis_index(PLANE)
    units = hidden.shape[1]

    other = lax.ppermute(hidden, "core", SWAP)
    both = jnp.concatenate([hidden, other], axis=0)
    blocks = {0: hidden}
    for hop in range(1, JUMP):
        blocks[hop] = lax.ppermute(blocks[hop - 1] if hop > 1 else both, LINE, step_pairs(1))

    p, q = lax.ppermute(hidden, LINE, step_pairs(JUMP)), lax.ppermute(other, LINE, step_pairs(JUMP))
    blocks[JUMP] = (p, q)
    for hop in range(JUMP + 1, HOPS + 1):
        p = lax.ppermute(p, LINE, step_pairs(1))
        q = lax.ppermute(q, LINE, step_pairs(1)) if hop < HOPS else None
        if hop == 6:
            p, q = after(p, blocks[2], cost=2000000000), after(q, cost=8000000000)
        blocks[hop] = (p, q)

    to = lax.rem(z + (1 - 2 * core) * t + NZ, NZ).astype(jnp.int32).reshape(1)
    part, turned = call(
        gram_kernel,
        [jax.ShapeDtypeStruct((NT, 8, 128), jnp.float32), jax.ShapeDtypeStruct((CHIP, SEQ), jnp.float32)],
        [to, hidden, out_grad], "grams", 2 * SEQ * SEQ * (units + D),
        scratch=[pltpu.VMEM(hidden.shape, hidden.dtype), pltpu.VMEM(out_grad.shape, out_grad.dtype),
                 pltpu.VMEM((384, SEQ), jnp.float32), pltpu.SemaphoreType.DMA, pltpu.SemaphoreType.DMA],
        far=True,
    )
    def clipped(parts):
        return call(
            clip_kernel,
            [jax.ShapeDtypeStruct((CHIP, SEQ), jnp.bfloat16), jax.ShapeDtypeStruct((8, 128), jnp.float32)],
            [live, parts, turned], "clip", 10000000000,
        )

    parts = lax.all_to_all(part, PLANE, 0, 0, tiled=False)
    block, norm = clipped(parts)
    block = lax.ppermute(block, ALL, spread_pairs())
    block = after(block, cost=4000000000)
    [spread] = call(spread_kernel, [jax.ShapeDtypeStruct((NT, CHIP, SEQ), jnp.bfloat16)], [block], "spread", 10000000000)
    s = lax.all_to_all(spread, PLANE, 0, 0, tiled=False)

    acc = matmul(s, blocks, range(0, 4), None)
    acc = matmul(s, blocks, range(4, HOPS), acc, 0)
    last = [(blocks[HOPS][0], HOPS)]
    row = core.astype(jnp.int32).reshape(1)
    theirs = lax.ppermute(last_products(1 - row, s, last, acc, 0), "core", SWAP)
    total = last_products(row, s, last, acc) + theirs
    grad = (total / math.sqrt(NZ * NC * SEQ)).T
    return grad, norm[0, 0:1]


def solution(mesh):
    grid = Mesh(mesh.devices.reshape(NZ, NC, NY, NX), ALL)
    return jax.shard_map(
        per_device,
        mesh=grid,
        in_specs=(P(LINE, PLANE), P(LINE, None), P(LINE)),
        out_specs=(P(PLANE, LINE), P(LINE)),
        check_vma=False,
    )
```
